32 devices in a mesh: seq: 4 (over y, x), tensor: 8 (over z, core).
Axes of the slice: x: 2, y: 2, z: 4, core: 2. Of those that a mesh axis runs over, the one named last changes fastest.
Arguments:
- tokens: bfloat16 [1024, 4096], P(('seq', 'tensor')), may hold values from -6 to 6
- w_gate: bfloat16 [4096, 8192], P('seq', 'tensor'), may hold values from -0.09375 to 0.09375
- w_xin: bfloat16 [4096, 8192], P('seq', 'tensor'), may hold values from -0.09375 to 0.09375
- w_bc: bfloat16 [4096, 2048], P('seq', 'tensor'), may hold values from -0.09375 to 0.09375
- w_dt: bfloat16 [4096, 128], P('seq', 'tensor'), may hold values from -0.09375 to 0.09375
- conv_x: float32 [4, 8192], P(None, 'tensor'), may hold values from -3 to 3
- conv_x_bias: float32 [8192], P('tensor'), may hold values from -3 to 3
- conv_bc: float32 [4, 2048], P(None, 'tensor'), may hold values from -3 to 3
- conv_bc_bias: float32 [2048], P('tensor'), may hold values from -3 to 3
- dt_bias: float32 [128], P('tensor'), may hold values from -1 to 1
- decay_rate: float32 [128], P('tensor'), may hold values from 0.000390625 to 0.08, as said below
- d_skip: float32 [128], P('tensor'), may hold values from 0.5 to 1.5
- norm_gain: float32 [8192], P('tensor'), may hold values from 0.25 to 1.75
- w_out: bfloat16 [8192, 4096], P('tensor', 'seq'), may hold values from -0.0625 to 0.0625
- lengths: int32 [8], replicated, may hold values from 1 to 512, 1024 in all
Outputs:
- mixed: bfloat16 [1024, 4096], P(('seq', 'tensor'))
The draws below stay inside these ranges and needn't reach their ends.
Inputs may be any that keep to these rules, and one draw needn't show every extreme that they name: lengths of 8 prompts that fill the pack of 1024 tokens exactly; the longest is exactly 512. `decay_rate`: positive rates.
All inputs are finite; a program needn't handle non-finite values.
Results may differ from the reference program's by a relative error of at most 0.03.
Values may be sent and summed in bfloat16 or wider, within the bound.
A program may use at most 64 MiB of HBM per device.

```python
import math
import jax
import jax.numpy as jnp
import numpy as np
from jax import lax

D = 4096
HEADS = 128
HDIM = 64
GROUPS = 8
STATE = 128
CONV = 4
STRETCH = 256
TOK_SPAN = 256
REQS = 8
INNER = 8192
TOKENS = 1024
MAXLEN = 512
INNER_DEV = 1024
N_TENSOR = 8


def draw_decay_rate(key, part):
    first, second, third = jax.random.split(key, 3)
    share = 0.5
    slowish = jax.random.uniform(first, (HEADS,)) < share
    slow_rate = jnp.exp(jax.random.uniform(second, (HEADS,), minval=jnp.log(0.2 / MAXLEN), maxval=jnp.log(1.0 / MAXLEN)))
    fast_rate = jnp.exp(jax.random.uniform(third, (HEADS,), minval=jnp.log(0.02), maxval=jnp.log(0.08)))
    return jnp.where(slowish, slow_rate, fast_rate).astype(jnp.float32)


def levels(rng, shape, cuts, low, largest):
    def one(dim, shards_of):
        steps = jax.random.uniform(jax.random.fold_in(jax.random.fold_in(rng, 6), dim), (shards_of,), jnp.float32, low / len(cuts), largest / len(cuts))
        return jnp.repeat(jnp.exp(steps), shape[dim] // shards_of).reshape((-1,) + (1,) * (len(shape) - dim - 1))

    loudness = one(*cuts[0])
    for cut in cuts[1:]:
        loudness = loudness * one(*cut)
    return loudness


def split_up(count, total, reach, slope):
    weights = [(1 << 20) // math.isqrt(grade ** slope) + 1 for grade in range(2, count + 1)]
    rest, holding = total - reach - (count - 1), [1] * (count - 1)
    while rest > 0:
        free = [i for i in range(count - 1) if holding[i] < reach]
        whole, remaining = sum([weights[i] for i in free]), rest
        for i in free:
            addition = min(reach - holding[i], max(1, remaining * weights[i] // whole), rest)
            holding[i] = holding[i] + addition
            rest = rest - addition
    return np.array([reach] + holding)


def ragged(stream_key, amount, total, most, lean):
    if amount == 2:
        one = jax.random.randint(stream_key, (), max(1, total - most), min(most, total - 1) + 1)
        return jnp.stack([one, total - one])
    sizes = jnp.asarray(split_up(amount, total, most, lean), jnp.int32)
    pairs = (amount - 1) // 2
    giver, taker = sizes[1:1 + 2 * pairs:2], sizes[2:2 + 2 * pairs:2]
    slack = jnp.minimum(giver - 1, most - taker)
    passed = jax.random.randint(jax.random.fold_in(stream_key, 1), (pairs,), 0, 1 << 20) % (slack + 1)
    sizes = sizes.at[1:1 + 2 * pairs:2].set(giver - passed).at[2:2 + 2 * pairs:2].set(taker + passed)
    return sizes[jax.random.permutation(jax.random.fold_in(stream_key, 2), amount)]


def scatter_about(key, extent, deviation, limit, cuts=(), held_as=jnp.bfloat16):
    values = deviation * jax.random.normal(key, extent, jnp.float32)
    if cuts:
        values = values * levels(key, extent, cuts, -0.22, 0.18)
    return jnp.clip(values, -limit, limit).astype(held_as)


def setup_inputs(seed: int = 0) -> dict:
    arg_keys = jax.random.split(jax.random.key(seed), 16)
    tokens = scatter_about(arg_keys[0], (TOKENS, D), 1.0, 6.0, ((0, 32),))
    w_gate = scatter_about(arg_keys[1], (D, INNER), D ** -0.5, 0.09375, ((0, 4), (1, 8)))
    w_xin = scatter_about(arg_keys[2], (D, INNER), D ** -0.5, 0.09375, ((0, 4), (1, 8)))
    w_bc = scatter_about(arg_keys[3], (D, 2 * GROUPS * STATE), D ** -0.5, 0.09375, ((0, 4), (1, 8)))
    w_dt = scatter_about(arg_keys[4], (D, HEADS), D ** -0.5, 0.09375, ((0, 4), (1, 8)))
    conv_x = scatter_about(arg_keys[5], (CONV, INNER), CONV ** -0.5, 3.0, ((1, 8),), jnp.float32)
    conv_x_bias = scatter_about(arg_keys[6], (INNER,), 0.5, 3.0, ((0, 8),), jnp.float32)
    conv_bc = scatter_about(arg_keys[7], (CONV, 2 * GROUPS * STATE), CONV ** -0.5, 3.0, ((1, 8),), jnp.float32)
    conv_bc_bias = scatter_about(arg_keys[8], (2 * GROUPS * STATE,), 0.5, 3.0, ((0, 8),), jnp.float32)
    dt_bias = jnp.clip(jax.random.uniform(arg_keys[9], (HEADS,), jnp.float32, -1.0, 1.0) * levels(arg_keys[9], (HEADS,), ((0, 8),), -0.4, 0.0), -1.0, 1.0)
    decay_rate = draw_decay_rate(jax.random.fold_in(arg_keys[15], 71), 0)
    d_skip = jnp.clip(0.5 + 1.0 * jax.random.uniform(arg_keys[11], (HEADS,), jnp.float32) ** levels(arg_keys[11], (HEADS,), ((0, 8),), -0.2, 0.2), 0.5, 1.5)
    norm_gain = jnp.clip(1.0 + 0.15 * jax.random.normal(arg_keys[12], (INNER,), jnp.float32), 0.25, 1.75)
    w_out = scatter_about(arg_keys[13], (INNER, D), INNER ** -0.5, 0.0625, ((0, 8), (1, 4)))
    lengths = ragged(arg_keys[14], REQS, TOKENS, MAXLEN, 2).astype(jnp.int32)
    return dict(tokens=tokens, w_gate=w_gate, w_xin=w_xin, w_bc=w_bc, w_dt=w_dt, conv_x=conv_x, conv_x_bias=conv_x_bias, conv_bc=conv_bc, conv_bc_bias=conv_bc_bias, dt_bias=dt_bias, decay_rate=decay_rate, d_skip=d_skip, norm_gain=norm_gain, w_out=w_out, lengths=lengths)


HIGH = lax.Precision.HIGHEST

def doc_ids(lengths, positions):
    starts = (jnp.cumsum(lengths) - lengths).astype(jnp.int32)
    counted = lax.optimization_barrier(jnp.sum((starts[None, :] <= positions[:, None]).astype(jnp.int32), axis=1))
    return (counted - 1).astype(jnp.int32)

def causal_conv(values, edge, weights, bias, docs, edge_docs):
    count = values.shape[0]
    extended = jnp.concatenate([edge, values], axis=0).astype(jnp.float32)
    all_docs = jnp.concatenate([edge_docs, docs])
    summed = jnp.zeros(values.shape, jnp.float32) + bias[None, :]
    for offset in range(weights.shape[0]):
        same = (all_docs[offset:offset + count] == docs).astype(jnp.float32)
        summed = summed + weights[offset][None, :] * extended[offset:offset + count] * same[:, None]
    return lax.optimization_barrier(jax.nn.silu(summed).astype(jnp.bfloat16))

def ssd_blocks(xvals, dtv, rate, bmat, cmat, docs, prev_doc, head_group, block):
    count, heads, hdim = xvals.shape
    nstate = bmat.shape[2]
    blocks = count // block
    logs = -dtv * rate[None, :]

    def split(array):
        return array.reshape((blocks, block) + array.shape[1:])
    lower = jnp.tril(jnp.ones((block, block), bool))

    def step(carry, pieces):
        state, last_doc = carry
        xblk, dblk, lblk, bblk, cblk, docblk = pieces
        cum = jnp.cumsum(lblk, axis=0)
        same = (docblk[:, None] == docblk[None, :]) & lower
        diff = cum.T[:, :, None] - cum.T[:, None, :]
        decay = jnp.exp(jnp.where(same[None], diff, -jnp.inf))
        scores = jnp.einsum('ign,jgn->gij', cblk, bblk, precision=HIGH)
        mixing = scores[head_group] * decay * dblk.T[:, None, :]
        inner = jnp.einsum('hij,jhp->ihp', mixing, xblk, precision=HIGH)
        open_in = (docblk == last_doc).astype(jnp.float32)
        carry_in = jnp.exp(cum) * open_in[:, None]
        chead = cblk[:, head_group, :]
        outer = jnp.einsum('ihn,hpn->ihp', chead, state, precision=HIGH) * carry_in[:, :, None]
        end_doc = docblk[-1]
        tail = jnp.exp(cum[-1][None, :] - cum) * (docblk == end_doc).astype(jnp.float32)[:, None] * dblk
        bhead = bblk[:, head_group, :]
        fresh = jnp.einsum('jh,jhp,jhn->hpn', tail, xblk, bhead, precision=HIGH)
        state = carry_in[-1][:, None, None] * state + fresh
        return ((state, end_doc), inner + outer)
    init = (jnp.zeros((heads, hdim, nstate), jnp.float32), prev_doc)
    (state, end_doc), outs = lax.scan(step, init, (split(xvals), split(dtv), split(logs), split(bmat), split(cmat), split(docs)))
    return (outs.reshape(count, heads, hdim), state)

def reference(tokens, w_gate, w_xin, w_bc, w_dt, conv_x, conv_x_bias, conv_bc, conv_bc_bias, dt_bias, decay_rate, d_skip, norm_gain, w_out, lengths):
    gate = jnp.dot(tokens, w_gate, preferred_element_type=jnp.float32).astype(jnp.bfloat16)
    xin = jnp.dot(tokens, w_xin, preferred_element_type=jnp.float32).astype(jnp.bfloat16)
    bcin = jnp.dot(tokens, w_bc, preferred_element_type=jnp.float32).astype(jnp.bfloat16)
    dtin = jnp.dot(tokens, w_dt, preferred_element_type=jnp.float32).astype(jnp.bfloat16)
    gate, xin, bcin, dtin = lax.optimization_barrier((gate, xin, bcin, dtin))
    positions = jnp.arange(TOKENS, dtype=jnp.int32)
    docs = doc_ids(lengths, positions)
    edge_docs = doc_ids(lengths, jnp.arange(-(CONV - 1), 0, dtype=jnp.int32))
    x_conv = causal_conv(xin, jnp.zeros((CONV - 1, INNER), jnp.bfloat16), conv_x, conv_x_bias, docs, edge_docs)
    bc_conv = causal_conv(bcin, jnp.zeros((CONV - 1, 2 * GROUPS * STATE), jnp.bfloat16), conv_bc, conv_bc_bias, docs, edge_docs)
    dtv = jax.nn.softplus(dtin.astype(jnp.float32) + dt_bias[None, :])
    xvals = x_conv.astype(jnp.float32).reshape(TOKENS, HEADS, HDIM)
    both = jnp.transpose(bc_conv.astype(jnp.float32).reshape(TOKENS, 2 * STATE, GROUPS), (0, 2, 1))
    bmat = both[:, :, :STATE]
    cmat = both[:, :, STATE:]
    head_group = np.arange(HEADS) // (HEADS // GROUPS)
    block = min(STRETCH, TOK_SPAN)
    ssd_out, last_state = ssd_blocks(xvals, dtv, decay_rate, bmat, cmat, docs, jnp.int32(-1), head_group, block)
    yvals = (ssd_out + d_skip[None, :, None] * xvals).reshape(TOKENS, INNER)
    gated = yvals * jax.nn.silu(gate.astype(jnp.float32))
    grouped = gated.reshape(TOKENS, GROUPS, INNER // GROUPS)
    scale = lax.rsqrt(lax.optimization_barrier(jnp.mean(grouped * grouped, axis=-1, keepdims=True)) + 1e-05)
    normed = ((grouped * scale).reshape(TOKENS, INNER) * norm_gain[None, :]).astype(jnp.bfloat16)

    def add_block(index, summed):
        begin = (index * INNER_DEV).astype(jnp.int32)
        rows = lax.dynamic_slice_in_dim(normed, begin, INNER_DEV, 1)
        wrows = lax.dynamic_slice_in_dim(w_out, begin, INNER_DEV, 0)
        part = jnp.dot(rows, wrows, preferred_element_type=jnp.float32).astype(jnp.bfloat16)
        return summed + lax.optimization_barrier(part).astype(jnp.float32)
    summed = lax.fori_loop(0, N_TENSOR, add_block, jnp.zeros((TOKENS, D), jnp.float32))
    return summed.astype(jnp.bfloat16)
```

```python
import jax
import jax.numpy as jnp
import numpy as np
from jax import lax
from jax.sharding import PartitionSpec as P

HDIM = 64
GROUPS = 8
STATE = 128
CONV = 4
STRETCH = 256
INNER = 8192


HIGH = lax.Precision.HIGHEST


def from_behind(x, axis, by):
    count = lax.axis_size(axis)
    pairs = [(i, i + by) for i in range(count) if 0 <= i + by < count]
    return lax.ppermute(x, axis, pairs)


def carried_in(x, axis, combine, identity):
    count, here = (lax.axis_size(axis), lax.axis_index(axis))
    everything = jax.tree.map(
        lambda part, kind: lax.all_gather(part.astype(kind), axis), x, (jnp.bfloat16, jnp.bfloat16)
    )
    start = jax.tree.map(
        lambda part, zero: jnp.broadcast_to(jnp.asarray(zero, part.dtype), part.shape), x, identity
    )

    def hop(k, before):
        reached = k < here
        new = combine(
            before, jax.tree.map(lambda part, own: part[k].astype(own.dtype), everything, x)
        )
        return jax.tree.map(lambda a, b: jnp.where(reached, a, b), new, before)

    return lax.fori_loop(0, count, hop, start)


def doc_ids(lengths, positions):
    starts = jnp.cumsum(lengths) - lengths
    counted = jnp.sum((starts[None, :] <= positions[:, None]).astype(jnp.int32), axis=1)
    return counted - 1


def causal_conv(values, edge, weights, bias, docs, edge_docs):
    count = values.shape[0]
    extended = jnp.concatenate([edge, values], axis=0).astype(jnp.float32)
    all_docs = jnp.concatenate([edge_docs, docs])
    summed = jnp.zeros(values.shape, jnp.float32) + bias[None, :]
    for offset in range(weights.shape[0]):
        same = (all_docs[offset : offset + count] == docs).astype(jnp.float32)
        summed = (
            summed + weights[offset][None, :] * extended[offset : offset + count] * same[:, None]
        )
    return lax.optimization_barrier(jax.nn.silu(summed).astype(jnp.bfloat16))


def ssd_blocks(xvals, dtv, rate, bmat, cmat, docs, prev_doc, head_group, block):
    count, heads, hdim = xvals.shape
    nstate = bmat.shape[2]
    blocks = count // block
    logs = -dtv * rate[None, :]

    def split(array):
        return array.reshape((blocks, block) + array.shape[1:])

    lower = jnp.tril(jnp.ones((block, block), bool))

    def step(carry, pieces):
        state, last_doc = carry
        xblk, dblk, lblk, bblk, cblk, docblk = pieces
        cum = jnp.cumsum(lblk, axis=0)
        same = (docblk[:, None] == docblk[None, :]) & lower
        diff = cum.T[:, :, None] - cum.T[:, None, :]
        decay = jnp.exp(jnp.where(same[None], diff, -jnp.inf))
        scores = jnp.einsum("ign,jgn->gij", cblk, bblk, precision=HIGH)
        mixing = scores[head_group] * decay * dblk.T[:, None, :]
        inner = jnp.einsum("hij,jhp->ihp", mixing, xblk, precision=HIGH)
        open_in = (docblk == last_doc).astype(jnp.float32)
        carry_in = jnp.exp(cum) * open_in[:, None]
        chead = cblk[:, head_group, :]
        outer = jnp.einsum("ihn,hpn->ihp", chead, state, precision=HIGH) * carry_in[:, :, None]
        end_doc = docblk[-1]
        tail = (
            jnp.exp(cum[-1][None, :] - cum)
            * (docblk == end_doc).astype(jnp.float32)[:, None]
            * dblk
        )
        bhead = bblk[:, head_group, :]
        fresh = jnp.einsum("jh,jhp,jhn->hpn", tail, xblk, bhead, precision=HIGH)
        state = carry_in[-1][:, None, None] * state + fresh
        return ((state, end_doc), inner + outer)

    init = (jnp.zeros((heads, hdim, nstate), jnp.float32), prev_doc)
    (state, end_doc), outs = lax.scan(
        step, init, (split(xvals), split(dtv), split(logs), split(bmat), split(cmat), split(docs))
    )
    return (outs.reshape(count, heads, hdim), state)


def shards_wide(
    tokens,
    w_gate,
    w_xin,
    w_bc,
    w_dt,
    conv_x,
    conv_x_bias,
    conv_bc,
    conv_bc_bias,
    dt_bias,
    decay_rate,
    d_skip,
    norm_gain,
    w_out,
    lengths,
):
    tensor_count = lax.axis_size("tensor")
    seq_index = lax.axis_index("seq")
    tensor_index = lax.axis_index("tensor")
    span_rows = lax.all_gather(tokens, "tensor", axis=0, tiled=True)
    span_len = span_rows.shape[0]
    pieces = (
        lax.all_gather(w_gate, "seq", axis=0, tiled=True),
        lax.all_gather(w_xin, "seq", axis=0, tiled=True),
        lax.all_gather(w_bc, "seq", axis=0, tiled=True),
        lax.all_gather(w_dt, "seq", axis=0, tiled=True),
    )
    gate_acc, xin_acc, bc_acc, dt_acc = tuple(
        (
            jnp.dot(span_rows, weight_piece, preferred_element_type=jnp.float32)
            for weight_piece in pieces
        )
    )
    gate = gate_acc.astype(jnp.bfloat16)
    xin = xin_acc.astype(jnp.bfloat16)
    bcin = bc_acc.astype(jnp.bfloat16)
    dtin = dt_acc.astype(jnp.bfloat16)
    gate, xin, bcin, dtin = lax.optimization_barrier((gate, xin, bcin, dtin))
    positions = seq_index * span_len + jnp.arange(span_len, dtype=jnp.int32)
    docs = doc_ids(lengths, positions)
    edge_docs = doc_ids(lengths, seq_index * span_len + jnp.arange(-(CONV - 1), 0, dtype=jnp.int32))
    prev_span_doc = doc_ids(lengths, positions[:1] - 1)[0]
    edge_x, edge_bc = from_behind(
        (xin[span_len - (CONV - 1) :], bcin[span_len - (CONV - 1) :]), "seq", 1
    )
    x_conv = causal_conv(xin, edge_x, conv_x, conv_x_bias, docs, edge_docs)
    bc_conv = causal_conv(bcin, edge_bc, conv_bc, conv_bc_bias, docs, edge_docs)
    group_span = tensor_count // GROUPS
    my_group = tensor_index // group_span
    every_group = lax.all_gather(bc_conv, "tensor", axis=1, tiled=True)
    arranged = every_group.reshape(span_len, 2 * STATE, GROUPS)
    group_cols = lax.dynamic_slice_in_dim(arranged, my_group, 1, 2).reshape(span_len, 2 * STATE)
    head_dev = w_dt.shape[1]
    head_group = np.zeros(head_dev, dtype=np.int32)
    both = group_cols.astype(jnp.float32)
    bmat = both[:, None, :STATE]
    cmat = both[:, None, STATE:]
    xvals = x_conv.astype(jnp.float32).reshape(span_len, head_dev, HDIM)
    dtv = jax.nn.softplus(dtin.astype(jnp.float32) + dt_bias[None, :])
    block = min(STRETCH, span_len)
    y_local, end_state = ssd_blocks(
        xvals, dtv, decay_rate, bmat, cmat, docs, prev_span_doc, head_group, block
    )
    cum_span = jnp.cumsum(-dtv * decay_rate[None, :], axis=0)
    open_span = (docs == prev_span_doc).astype(jnp.float32)
    span_decay = jnp.exp(cum_span[-1]) * open_span[-1]

    def combine(earlier, later):
        return (earlier[0] * later[0], later[0][:, None, None] * earlier[1] + later[1])

    entering = carried_in(
        (span_decay, end_state),
        "seq",
        combine,
        (jnp.ones_like(span_decay), jnp.zeros_like(end_state)),
    )[1]
    carried = jnp.exp(cum_span) * open_span[:, None]
    y_enter = (
        jnp.einsum("ihn,hpn->ihp", cmat[:, head_group, :], entering, precision=HIGH)
        * carried[:, :, None]
    )
    yvals = (y_local + y_enter + d_skip[None, :, None] * xvals).reshape(span_len, head_dev * HDIM)
    gated = yvals * jax.nn.silu(gate.astype(jnp.float32))
    local_sq = jnp.sum(gated * gated, axis=1)
    group_mark = (jnp.arange(GROUPS) == my_group).astype(jnp.float32)
    every_sum = lax.psum(local_sq[:, None] * group_mark[None, :], "tensor")
    group_mean = jnp.sum(every_sum * group_mark[None, :], axis=1) / (INNER // GROUPS)
    normed = (gated * lax.rsqrt(group_mean + 1e-05)[:, None] * norm_gain[None, :]).astype(
        jnp.bfloat16
    )
    w_full = lax.all_gather(w_out, "seq", axis=1, tiled=True)
    return lax.psum_scatter(
        jnp.dot(normed, w_full, preferred_element_type=jnp.float32).astype(jnp.bfloat16),
        "tensor",
        scatter_dimension=0,
        tiled=True,
    )


def conv_full(values, weights, bias, docs, axis):
    count = values.shape[axis]
    values = values.astype(jnp.float32)

    def along(vector):
        return vector[:, None] if axis == 0 else vector[None, :]

    def across(vector):
        return vector[None, :] if axis == 0 else vector[:, None]

    summed = across(weights[CONV - 1]) * values + across(bias)
    for back in range(1, CONV):
        kept = lax.slice_in_dim(values, 0, count - back, axis=axis)
        pad = [(0, 0), (0, 0)]
        pad[axis] = (back, 0)
        same = jnp.concatenate(
            [jnp.zeros((back,), jnp.float32), (docs[:-back] == docs[back:]).astype(jnp.float32)]
        )
        summed = summed + across(weights[CONV - 1 - back]) * jnp.pad(kept, pad) * along(same)
    return jax.nn.silu(summed).astype(jnp.bfloat16)


def scan_heads(xc, dtv, rate, bmat, cmat, docs, block):
    count, heads = dtv.shape
    blocks = count // block
    xh = xc.reshape(blocks, block, heads, HDIM)
    dtb = dtv.reshape(blocks, block, heads)
    cum = jnp.cumsum(-dtb * rate[None, None, :], axis=1)
    docb = docs.reshape(blocks, block)
    bb = bmat.reshape(STATE, blocks, block)
    cb = cmat.reshape(STATE, blocks, block)
    scores = jnp.einsum("nbi,nbj->bij", cb, bb, preferred_element_type=jnp.float32)
    lower = jnp.tril(jnp.ones((block, block), bool))
    same = (docb[:, :, None] == docb[:, None, :]) & lower[None]
    cumt = cum.transpose(0, 2, 1)
    diff = cumt[:, :, :, None] - cumt[:, :, None, :]
    decay = jnp.exp(jnp.where(same[:, None], diff, -jnp.inf))
    mixing = scores[:, None] * decay * dtb.transpose(0, 2, 1)[:, :, None, :]
    inner = jnp.einsum(
        "bhij,bjhp->bihp", mixing.astype(jnp.bfloat16), xh, preferred_element_type=jnp.float32
    )
    end_doc = docb[:, -1]
    last_doc = jnp.concatenate([jnp.full((1,), -1, docs.dtype), end_doc[:-1]])
    carry_in = jnp.exp(cum) * (docb == last_doc[:, None]).astype(jnp.float32)[:, :, None]
    tail = jnp.exp(cum[:, -1:] - cum) * (docb == end_doc[:, None]).astype(jnp.float32)[:, :, None] * dtb
    tx = (tail[..., None] * xh.astype(jnp.float32)).astype(jnp.bfloat16)
    fresh = jnp.einsum("bjhp,nbj->bhpn", tx, bb, preferred_element_type=jnp.float32)
    states = [jnp.zeros((heads, HDIM, STATE), jnp.float32)]
    for k in range(blocks - 1):
        states.append(carry_in[k, -1][:, None, None] * states[-1] + fresh[k])
    entering = jnp.stack(states).astype(jnp.bfloat16)
    outer = jnp.einsum("nbi,bhpn->bihp", cb, entering, preferred_element_type=jnp.float32)
    return (inner + outer * carry_in[..., None]).reshape(count, heads * HDIM)


def shards(
    tokens,
    w_gate,
    w_xin,
    w_bc,
    w_dt,
    conv_x,
    conv_x_bias,
    conv_bc,
    conv_bc_bias,
    dt_bias,
    decay_rate,
    d_skip,
    norm_gain,
    w_out,
    lengths,
):
    seqs = lax.axis_size("seq")
    tens = lax.axis_size("tensor")
    here = lax.axis_index("seq")
    own, depth = tokens.shape[0], w_gate.shape[0]
    total = own * seqs * tens
    chans = w_gate.shape[1] // seqs
    heads = w_dt.shape[1] // seqs
    parts = w_bc.shape[1] // (seqs * GROUPS)
    columns = lax.all_to_all(tokens, "seq", 1, 0, tiled=True)
    rows = lax.all_gather(columns, "tensor", axis=0)
    rows = rows.reshape(tens, seqs, own, depth).transpose(1, 0, 2, 3).reshape(total, depth)

    def project(weight):
        return jnp.dot(rows, weight, preferred_element_type=jnp.float32).astype(jnp.bfloat16)

    gate = lax.psum_scatter(project(w_gate), "seq", scatter_dimension=1, tiled=True)
    xin = lax.psum_scatter(project(w_xin), "seq", scatter_dimension=1, tiled=True)
    small = jnp.concatenate(
        [
            w_bc.T.reshape(seqs, parts, GROUPS, depth)
            .transpose(0, 2, 1, 3)
            .reshape(seqs, parts * GROUPS, depth),
            w_dt.T.reshape(seqs, heads, depth),
        ],
        axis=1,
    )
    small = jnp.einsum("scd,td->sct", small, rows, preferred_element_type=jnp.float32)
    small = lax.psum_scatter(small.astype(jnp.bfloat16), "seq", scatter_dimension=0, tiled=True)[0]
    docs = doc_ids(lengths, jnp.arange(total, dtype=jnp.int32))

    def mine(vector, width, axis=0):
        return lax.dynamic_slice_in_dim(vector, here * width, width, axis)

    xc = conv_full(xin, mine(conv_x, chans, 1), mine(conv_x_bias, chans), docs, 0)

    def grouped(vector):
        lead = vector.shape[:-1]
        vector = mine(vector, parts * GROUPS, len(lead)).reshape(lead + (parts, GROUPS))
        return jnp.swapaxes(vector, -1, -2).reshape(lead + (parts * GROUPS,))

    bcc = conv_full(small[: parts * GROUPS], grouped(conv_bc), grouped(conv_bc_bias), docs, 1)
    bcc = lax.all_to_all(bcc.reshape(GROUPS, parts, total), "tensor", 0, 0, tiled=True)
    bcc = lax.all_gather(bcc, "seq", axis=0).transpose(1, 0, 2, 3).reshape(2 * STATE, total)
    dtin = small[parts * GROUPS :].T.astype(jnp.float32)
    dtv = jax.nn.softplus(dtin + mine(dt_bias, heads)[None, :])
    y = scan_heads(
        xc, dtv, mine(decay_rate, heads), bcc[:STATE], bcc[STATE:], docs, min(STRETCH, total)
    )
    y = y + jnp.repeat(mine(d_skip, heads), HDIM)[None, :] * xc.astype(jnp.float32)
    gated = (y * jax.nn.silu(gate.astype(jnp.float32))).astype(jnp.bfloat16)
    gated = lax.all_gather(gated, "seq", axis=1, tiled=True).astype(jnp.float32)
    mean = jnp.mean(gated * gated, axis=1, keepdims=True)
    normed = (gated * lax.rsqrt(mean + 1e-05) * norm_gain[None, :]).astype(jnp.bfloat16)
    out = jnp.dot(normed, w_out, preferred_element_type=jnp.float32).astype(jnp.bfloat16)
    out = out.reshape(seqs, tens, own, depth).transpose(1, 0, 2, 3)
    out = lax.psum_scatter(out, "tensor", scatter_dimension=0, tiled=True)[0]
    return lax.all_to_all(out, "seq", 0, 2, tiled=True)[0]


def solution(mesh):
    seqs, tens = mesh.shape["seq"], mesh.shape["tensor"]
    heads = INNER // HDIM
    narrow = tens == GROUPS and heads % (seqs * tens) == 0 and 2 * STATE % (seqs * tens) == 0
    body = shards if narrow else shards_wide
    in_specs = (
        P(("seq", "tensor"), None),
        P("seq", "tensor"),
        P("seq", "tensor"),
        P("seq", "tensor"),
        P("seq", "tensor"),
        P(None, "tensor"),
        P("tensor"),
        P(None, "tensor"),
        P("tensor"),
        P("tensor"),
        P("tensor"),
        P("tensor"),
        P("tensor"),
        P("tensor", "seq"),
        P(),
    )
    out_specs = P(("seq", "tensor"), None)
    return jax.shard_map(body, mesh=mesh, in_specs=in_specs, out_specs=out_specs, check_vma=False)
```

```python
import jax
import jax.numpy as jnp
import numpy as np
from jax import lax
from jax.experimental import pallas as pl
from jax.experimental.pallas import tpu as pltpu
from jax.sharding import PartitionSpec as P

HDIM = 64
GROUPS = 8
STATE = 128
CONV = 4
STRETCH = 256
INNER = 8192


HIGH = lax.Precision.HIGHEST


def from_behind(x, axis, by):
    count = lax.axis_size(axis)
    pairs = [(i, i + by) for i in range(count) if 0 <= i + by < count]
    return lax.ppermute(x, axis, pairs)


def carried_in(x, axis, combine, identity):
    count, here = (lax.axis_size(axis), lax.axis_index(axis))
    everything = jax.tree.map(
        lambda part, kind: lax.all_gather(part.astype(kind), axis), x, (jnp.bfloat16, jnp.bfloat16)
    )
    start = jax.tree.map(
        lambda part, zero: jnp.broadcast_to(jnp.asarray(zero, part.dtype), part.shape), x, identity
    )

    def hop(k, before):
        reached = k < here
        new = combine(
            before, jax.tree.map(lambda part, own: part[k].astype(own.dtype), everything, x)
        )
        return jax.tree.map(lambda a, b: jnp.where(reached, a, b), new, before)

    return lax.fori_loop(0, count, hop, start)


def doc_ids(lengths, positions):
    starts = jnp.cumsum(lengths) - lengths
    counted = jnp.sum((starts[None, :] <= positions[:, None]).astype(jnp.int32), axis=1)
    return counted - 1


def causal_conv(values, edge, weights, bias, docs, edge_docs):
    count = values.shape[0]
    extended = jnp.concatenate([edge, values], axis=0).astype(jnp.float32)
    all_docs = jnp.concatenate([edge_docs, docs])
    summed = jnp.zeros(values.shape, jnp.float32) + bias[None, :]
    for offset in range(weights.shape[0]):
        same = (all_docs[offset : offset + count] == docs).astype(jnp.float32)
        summed = (
            summed + weights[offset][None, :] * extended[offset : offset + count] * same[:, None]
        )
    return lax.optimization_barrier(jax.nn.silu(summed).astype(jnp.bfloat16))


def ssd_blocks(xvals, dtv, rate, bmat, cmat, docs, prev_doc, head_group, block):
    count, heads, hdim = xvals.shape
    nstate = bmat.shape[2]
    blocks = count // block
    logs = -dtv * rate[None, :]

    def split(array):
        return array.reshape((blocks, block) + array.shape[1:])

    lower = jnp.tril(jnp.ones((block, block), bool))

    def step(carry, pieces):
        state, last_doc = carry
        xblk, dblk, lblk, bblk, cblk, docblk = pieces
        cum = jnp.cumsum(lblk, axis=0)
        same = (docblk[:, None] == docblk[None, :]) & lower
        diff = cum.T[:, :, None] - cum.T[:, None, :]
        decay = jnp.exp(jnp.where(same[None], diff, -jnp.inf))
        scores = jnp.einsum("ign,jgn->gij", cblk, bblk, precision=HIGH)
        mixing = scores[head_group] * decay * dblk.T[:, None, :]
        inner = jnp.einsum("hij,jhp->ihp", mixing, xblk, precision=HIGH)
        open_in = (docblk == last_doc).astype(jnp.float32)
        carry_in = jnp.exp(cum) * open_in[:, None]
        chead = cblk[:, head_group, :]
        outer = jnp.einsum("ihn,hpn->ihp", chead, state, precision=HIGH) * carry_in[:, :, None]
        end_doc = docblk[-1]
        tail = (
            jnp.exp(cum[-1][None, :] - cum)
            * (docblk == end_doc).astype(jnp.float32)[:, None]
            * dblk
        )
        bhead = bblk[:, head_group, :]
        fresh = jnp.einsum("jh,jhp,jhn->hpn", tail, xblk, bhead, precision=HIGH)
        state = carry_in[-1][:, None, None] * state + fresh
        return ((state, end_doc), inner + outer)

    init = (jnp.zeros((heads, hdim, nstate), jnp.float32), prev_doc)
    (state, end_doc), outs = lax.scan(
        step, init, (split(xvals), split(dtv), split(logs), split(bmat), split(cmat), split(docs))
    )
    return (outs.reshape(count, heads, hdim), state)


def shards_wide(
    tokens,
    w_gate,
    w_xin,
    w_bc,
    w_dt,
    conv_x,
    conv_x_bias,
    conv_bc,
    conv_bc_bias,
    dt_bias,
    decay_rate,
    d_skip,
    norm_gain,
    w_out,
    lengths,
):
    tensor_count = lax.axis_size("tensor")
    seq_index = lax.axis_index("seq")
    tensor_index = lax.axis_index("tensor")
    span_rows = lax.all_gather(tokens, "tensor", axis=0, tiled=True)
    span_len = span_rows.shape[0]
    pieces = (
        lax.all_gather(w_gate, "seq", axis=0, tiled=True),
        lax.all_gather(w_xin, "seq", axis=0, tiled=True),
        lax.all_gather(w_bc, "seq", axis=0, tiled=True),
        lax.all_gather(w_dt, "seq", axis=0, tiled=True),
    )
    gate_acc, xin_acc, bc_acc, dt_acc = tuple(
        (
            jnp.dot(span_rows, weight_piece, preferred_element_type=jnp.float32)
            for weight_piece in pieces
        )
    )
    gate = gate_acc.astype(jnp.bfloat16)
    xin = xin_acc.astype(jnp.bfloat16)
    bcin = bc_acc.astype(jnp.bfloat16)
    dtin = dt_acc.astype(jnp.bfloat16)
    gate, xin, bcin, dtin = lax.optimization_barrier((gate, xin, bcin, dtin))
    positions = seq_index * span_len + jnp.arange(span_len, dtype=jnp.int32)
    docs = doc_ids(lengths, positions)
    edge_docs = doc_ids(lengths, seq_index * span_len + jnp.arange(-(CONV - 1), 0, dtype=jnp.int32))
    prev_span_doc = doc_ids(lengths, positions[:1] - 1)[0]
    edge_x, edge_bc = from_behind(
        (xin[span_len - (CONV - 1) :], bcin[span_len - (CONV - 1) :]), "seq", 1
    )
    x_conv = causal_conv(xin, edge_x, conv_x, conv_x_bias, docs, edge_docs)
    bc_conv = causal_conv(bcin, edge_bc, conv_bc, conv_bc_bias, docs, edge_docs)
    group_span = tensor_count // GROUPS
    my_group = tensor_index // group_span
    every_group = lax.all_gather(bc_conv, "tensor", axis=1, tiled=True)
    arranged = every_group.reshape(span_len, 2 * STATE, GROUPS)
    group_cols = lax.dynamic_slice_in_dim(arranged, my_group, 1, 2).reshape(span_len, 2 * STATE)
    head_dev = w_dt.shape[1]
    head_group = np.zeros(head_dev, dtype=np.int32)
    both = group_cols.astype(jnp.float32)
    bmat = both[:, None, :STATE]
    cmat = both[:, None, STATE:]
    xvals = x_conv.astype(jnp.float32).reshape(span_len, head_dev, HDIM)
    dtv = jax.nn.softplus(dtin.astype(jnp.float32) + dt_bias[None, :])
    block = min(STRETCH, span_len)
    y_local, end_state = ssd_blocks(
        xvals, dtv, decay_rate, bmat, cmat, docs, prev_span_doc, head_group, block
    )
    cum_span = jnp.cumsum(-dtv * decay_rate[None, :], axis=0)
    open_span = (docs == prev_span_doc).astype(jnp.float32)
    span_decay = jnp.exp(cum_span[-1]) * open_span[-1]

    def combine(earlier, later):
        return (earlier[0] * later[0], later[0][:, None, None] * earlier[1] + later[1])

    entering = carried_in(
        (span_decay, end_state),
        "seq",
        combine,
        (jnp.ones_like(span_decay), jnp.zeros_like(end_state)),
    )[1]
    carried = jnp.exp(cum_span) * open_span[:, None]
    y_enter = (
        jnp.einsum("ihn,hpn->ihp", cmat[:, head_group, :], entering, precision=HIGH)
        * carried[:, :, None]
    )
    yvals = (y_local + y_enter + d_skip[None, :, None] * xvals).reshape(span_len, head_dev * HDIM)
    gated = yvals * jax.nn.silu(gate.astype(jnp.float32))
    local_sq = jnp.sum(gated * gated, axis=1)
    group_mark = (jnp.arange(GROUPS) == my_group).astype(jnp.float32)
    every_sum = lax.psum(local_sq[:, None] * group_mark[None, :], "tensor")
    group_mean = jnp.sum(every_sum * group_mark[None, :], axis=1) / (INNER // GROUPS)
    normed = (gated * lax.rsqrt(group_mean + 1e-05)[:, None] * norm_gain[None, :]).astype(
        jnp.bfloat16
    )
    w_full = lax.all_gather(w_out, "seq", axis=1, tiled=True)
    return lax.psum_scatter(
        jnp.dot(normed, w_full, preferred_element_type=jnp.float32).astype(jnp.bfloat16),
        "tensor",
        scatter_dimension=0,
        tiled=True,
    )


def enter(peers):
    barrier = pltpu.get_barrier_semaphore()
    for peer in peers:
        pl.semaphore_signal(barrier, inc=1, device_id=peer, device_id_type=pl.DeviceIdType.MESH)
    pl.semaphore_wait(barrier, len(peers))


def remote(src, dst, send, recv, peer):
    return pltpu.make_async_remote_copy(
        src_ref=src,
        dst_ref=dst,
        send_sem=send,
        recv_sem=recv,
        device_id=peer,
        device_id_type=pl.DeviceIdType.MESH,
    )


def places():
    s, t = lax.axis_index("seq"), lax.axis_index("tensor")
    seqs, chips = lax.axis_size("seq"), lax.axis_size("tensor") // 2
    z, c = t // 2, t % 2

    def along(ds, dz):
        return lax.rem(s + ds, seqs), lax.rem(z + dz, chips)

    return s, z, c, seqs, chips, along


def out_kernel(
    g_ref, gain_ref, w_ref, out_ref, held, normed, part, sib, pair, got,
    g_send, g_recv, p_send, p_recv, o_send, o_recv,
):
    s, z, c, seqs, chips, along = places()
    span = g_ref.shape[0] // seqs
    width = g_ref.shape[1]
    own = out_ref.shape[0]
    cols = w_ref.shape[1]
    sibling = (s, 2 * z + 1 - c)
    offsets = [(ds, dz) for ds in range(seqs) for dz in range(chips) if ds or dz]
    enter([(along(ds, dz)[0], 2 * along(ds, dz)[1] + c) for ds, dz in offsets] + [sibling])
    order = list(range(1, seqs)) + [0]
    gathers = {}
    for k in order:
        for ds in range(1, seqs):
            rows = pl.ds(pl.multiple_of(lax.rem(s + ds + k, seqs) * span, span), span)
            gathers[k, ds] = remote(
                g_ref.at[rows],
                held.at[ds, rows],
                g_send.at[k, ds],
                g_recv.at[k, ds],
                (along(ds, 0)[0], 2 * z + c),
            )
            gathers[k, ds].start()
    pairs, sends = {}, []

    def finish(k):
        q = lax.rem(s + k, seqs)
        pairs[k].wait_recv()
        for dz in range(chips):
            there = along(0, dz)[1]
            both = part[q, there, c].astype(jnp.float32) + sib[q, there].astype(jnp.float32)
            if k == 0 and dz == 0:
                got[0, 0] = both.astype(jnp.bfloat16)
            else:
                pair[k, dz] = both.astype(jnp.bfloat16)
                sends.append(
                    remote(
                        pair.at[k, dz],
                        got.at[k, dz],
                        o_send.at[k, dz],
                        o_recv.at[k, dz],
                        (q, 2 * there + c),
                    )
                )
                sends[-1].start()

    for step, k in enumerate(order):
        q = lax.rem(s + k, seqs)
        rows = pl.ds(pl.multiple_of(q * span, span), span)
        for ds in range(1, seqs):
            gathers[k, ds].wait_recv()
        blocks = [g_ref[rows, :].astype(jnp.float32)] + [
            held[ds, rows, :].astype(jnp.float32) for ds in range(1, seqs)
        ]
        squares = blocks[0] * blocks[0]
        for b in blocks[1:]:
            squares = squares + b * b
        scale = lax.rsqrt(jnp.sum(squares, axis=1, keepdims=True) / (width * seqs) + 1e-05)
        froms = [pl.multiple_of(lax.rem(s + seqs - ds, seqs) * width, width) for ds in range(seqs)]
        for ds in range(seqs):
            normed[ds] = (blocks[ds] * scale * gain_ref[:, pl.ds(froms[ds], width)]).astype(
                jnp.bfloat16
            )
        tile = 256

        def column(n, _):
            here = pl.ds(pl.multiple_of(n * tile, tile), tile)
            acc = jnp.zeros((span, tile), jnp.float32)
            for ds in range(seqs):
                acc = acc + jnp.dot(
                    normed[ds],
                    w_ref[pl.ds(froms[ds], width), here],
                    preferred_element_type=jnp.float32,
                )
            part[q, :, :, :, here] = acc.astype(jnp.bfloat16).reshape(chips, 2, own, tile)
            return 0

        lax.fori_loop(0, cols // tile, column, 0)
        pairs[k] = remote(
            part.at[q, :, 1 - c], sib.at[q], p_send.at[k], p_recv.at[k], sibling
        )
        pairs[k].start()
        if step:
            finish(order[step - 1])
    finish(order[-1])
    for copy in sends:
        copy.wait_recv()
    for ds in range(seqs):
        total = got[ds, 0].astype(jnp.float32)
        for dz in range(1, chips):
            total = total + got[ds, dz].astype(jnp.float32)
        begin = pl.multiple_of(lax.rem(s + seqs - ds, seqs) * cols, cols)
        out_ref[:, pl.ds(begin, cols)] = total.astype(jnp.bfloat16)
    for copy in list(gathers.values()) + list(pairs.values()) + sends:
        copy.wait_send()


def project_out(gated, gain, w_out, own, seqs, chips):
    total, width = gated.shape
    cols = w_out.shape[1]
    dma = pltpu.SemaphoreType.DMA
    vmem = pl.BlockSpec(memory_space=pltpu.VMEM)
    return pl.pallas_call(
        out_kernel,
        out_shape=jax.ShapeDtypeStruct((own, cols * seqs), jnp.bfloat16),
        in_specs=[vmem] * 3,
        out_specs=vmem,
        scratch_shapes=[
            pltpu.VMEM((seqs, total, width), jnp.bfloat16),
            pltpu.VMEM((seqs, total // seqs, width), jnp.bfloat16),
            pltpu.VMEM((seqs, chips, 2, own, cols), jnp.bfloat16),
            pltpu.VMEM((seqs, chips, own, cols), jnp.bfloat16),
            pltpu.VMEM((seqs, chips, own, cols), jnp.bfloat16),
            pltpu.VMEM((seqs, chips, own, cols), jnp.bfloat16),
            dma((seqs, seqs)),
            dma((seqs, seqs)),
            dma((seqs,)),
            dma((seqs,)),
            dma((seqs, chips)),
            dma((seqs, chips)),
        ],
        compiler_params=pltpu.CompilerParams(
            collective_id=1, has_side_effects=True, vmem_limit_bytes=40 * 2**20
        ),
    )(gated, gain[None, :], w_out)


def in_kernel(
    tok_ref, wg_ref, wx_ref, ws_ref, gate_ref, xin_ref, small_ref,
    tok, mine, mine_s, sent, sent_s, got, got_s,
    t_send, t_recv, f_send, f_recv, p_send, p_recv, q_send, q_recv,
):
    s, z, c, seqs, chips, along = places()
    own = tok_ref.shape[0]
    depth = wg_ref.shape[0]
    width = wg_ref.shape[1] // seqs
    span = own * chips * 2
    sibling = (s, 2 * z + 1 - c)
    offsets = [(ds, dz) for ds in range(seqs) for dz in range(chips) if ds or dz]
    enter([(along(ds, dz)[0], 2 * along(ds, dz)[1] + c) for ds, dz in offsets] + [sibling])
    spread = {}
    for ds, dz in offsets:
        to, there = along(ds, dz)
        spread[ds, dz] = remote(
            tok_ref.at[:, pl.ds(pl.multiple_of(to * depth, depth), depth)],
            tok.at[ds, z, c],
            t_send.at[ds, dz],
            t_recv.at[ds, dz],
            (to, 2 * there + c),
        )
        spread[ds, dz].start()
    tok[0, z, c] = tok_ref[:, pl.ds(pl.multiple_of(s * depth, depth), depth)]
    forwards, sums = [], []

    def forward(k):
        for ds, dz in offsets:
            if ds == k:
                spread[ds, dz].wait_recv()
        forwards.append(
            remote(tok.at[k, :, c], tok.at[k, :, c], f_send.at[k], f_recv.at[k], sibling)
        )
        forwards[k].start()

    forward(0)
    for k in range(seqs):
        forwards[k].wait_recv()
        if k + 1 < seqs:
            forward(k + 1)
        q = lax.rem(s + seqs - k, seqs)
        for ds in list(range(1, seqs)) + [0]:
            to = along(ds, 0)[0]
            cols = pl.ds(pl.multiple_of(to * width, width), width)
            rows = tok[k].reshape(span, depth)
            gate = jnp.dot(rows, wg_ref[:, cols], preferred_element_type=jnp.float32)
            xin = jnp.dot(rows, wx_ref[:, cols], preferred_element_type=jnp.float32)
            small = lax.dot_general(
                ws_ref[to], rows, (((1,), (1,)), ((), ())), preferred_element_type=jnp.float32
            )
            if ds == 0:
                mine[q, :, :width] = gate
                mine[q, :, width:] = xin
                mine_s[q] = small
                continue
            sent[ds, k, :, :width] = gate.astype(jnp.bfloat16)
            sent[ds, k, :, width:] = xin.astype(jnp.bfloat16)
            sent_s[ds, k] = small.astype(jnp.bfloat16)
            peer = (to, 2 * z + c)
            for copy in (
                remote(sent.at[ds, k], got.at[ds, q], p_send.at[ds, k], p_recv.at[ds, k], peer),
                remote(
                    sent_s.at[ds, k], got_s.at[ds, q], q_send.at[ds, k], q_recv.at[ds, k], peer
                ),
            ):
                copy.start()
                sums.append(copy)
    for copy in sums:
        copy.wait_recv()

    def add(q, _):
        rows = pl.ds(pl.multiple_of(q * span, span), span)
        total, small = mine[q], mine_s[q]
        for ds in range(1, seqs):
            total = total + got[ds, q].astype(jnp.float32)
            small = small + got_s[ds, q].astype(jnp.float32)
        gate_ref[rows, :] = total[:, :width].astype(jnp.bfloat16)
        xin_ref[rows, :] = total[:, width:].astype(jnp.bfloat16)
        small_ref[:, rows] = small.astype(jnp.bfloat16)
        return 0

    lax.fori_loop(0, seqs, add, 0)
    for copy in list(spread.values()) + forwards + sums:
        copy.wait_send()


def project_in(tokens, w_gate, w_xin, w_small, seqs, chips):
    own = tokens.shape[0]
    depth = w_gate.shape[0]
    width = w_gate.shape[1] // seqs
    span = own * chips * 2
    few = w_small.shape[1]
    dma = pltpu.SemaphoreType.DMA
    vmem = pl.BlockSpec(memory_space=pltpu.VMEM)
    return pl.pallas_call(
        in_kernel,
        out_shape=(
            jax.ShapeDtypeStruct((span * seqs, width), jnp.bfloat16),
            jax.ShapeDtypeStruct((span * seqs, width), jnp.bfloat16),
            jax.ShapeDtypeStruct((few, span * seqs), jnp.bfloat16),
        ),
        in_specs=[vmem] * 4,
        out_specs=(vmem,) * 3,
        scratch_shapes=[
            pltpu.VMEM((seqs, chips, 2, own, depth), jnp.bfloat16),
            pltpu.VMEM((seqs, span, 2 * width), jnp.float32),
            pltpu.VMEM((seqs, few, span), jnp.float32),
            pltpu.VMEM((seqs, seqs, span, 2 * width), jnp.bfloat16),
            pltpu.VMEM((seqs, seqs, few, span), jnp.bfloat16),
            pltpu.VMEM((seqs, seqs, span, 2 * width), jnp.bfloat16),
            pltpu.VMEM((seqs, seqs, few, span), jnp.bfloat16),
            dma((seqs, chips)),
            dma((seqs, chips)),
            dma((seqs,)),
            dma((seqs,)),
            dma((seqs, seqs)),
            dma((seqs, seqs)),
            dma((seqs, seqs)),
            dma((seqs, seqs)),
        ],
        compiler_params=pltpu.CompilerParams(
            collective_id=2, has_side_effects=True, vmem_limit_bytes=48 * 2**20
        ),
    )(tokens, w_gate, w_xin, w_small)


def conv_full(values, weights, bias, docs, axis):
    count = values.shape[axis]
    values = values.astype(jnp.float32)

    def along(vector):
        return vector[:, None] if axis == 0 else vector[None, :]

    def across(vector):
        return vector[None, :] if axis == 0 else vector[:, None]

    summed = across(weights[CONV - 1]) * values + across(bias)
    for back in range(1, CONV):
        kept = lax.slice_in_dim(values, 0, count - back, axis=axis)
        pad = [(0, 0), (0, 0)]
        pad[axis] = (back, 0)
        same = jnp.concatenate(
            [jnp.zeros((back,), jnp.float32), (docs[:-back] == docs[back:]).astype(jnp.float32)]
        )
        summed = summed + across(weights[CONV - 1 - back]) * jnp.pad(kept, pad) * along(same)
    return jax.nn.silu(summed).astype(jnp.bfloat16)


def scan_heads(xc, dtv, rate, bmat, cmat, docs, block):
    count, heads = dtv.shape
    blocks = count // block
    xh = xc.reshape(blocks, block, heads, HDIM)
    dtb = dtv.reshape(blocks, block, heads)
    cum = jnp.cumsum(-dtb * rate[None, None, :], axis=1)
    docb = docs.reshape(blocks, block)
    bb = bmat.reshape(STATE, blocks, block)
    cb = cmat.reshape(STATE, blocks, block)
    scores = jnp.einsum("nbi,nbj->bij", cb, bb, preferred_element_type=jnp.float32)
    lower = jnp.tril(jnp.ones((block, block), bool))
    same = (docb[:, :, None] == docb[:, None, :]) & lower[None]
    cumt = cum.transpose(0, 2, 1)
    diff = cumt[:, :, :, None] - cumt[:, :, None, :]
    decay = jnp.exp(jnp.where(same[:, None], diff, -jnp.inf))
    mixing = scores[:, None] * decay * dtb.transpose(0, 2, 1)[:, :, None, :]
    inner = jnp.einsum(
        "bhij,bjhp->bihp", mixing.astype(jnp.bfloat16), xh, preferred_element_type=jnp.float32
    )
    end_doc = docb[:, -1]
    last_doc = jnp.concatenate([jnp.full((1,), -1, docs.dtype), end_doc[:-1]])
    carry_in = jnp.exp(cum) * (docb == last_doc[:, None]).astype(jnp.float32)[:, :, None]
    tail = jnp.exp(cum[:, -1:] - cum) * (docb == end_doc[:, None]).astype(jnp.float32)[:, :, None] * dtb
    tx = (tail[..., None] * xh.astype(jnp.float32)).astype(jnp.bfloat16)
    fresh = jnp.einsum("bjhp,nbj->bhpn", tx, bb, preferred_element_type=jnp.float32)
    states = [jnp.zeros((heads, HDIM, STATE), jnp.float32)]
    for k in range(blocks - 1):
        states.append(carry_in[k, -1][:, None, None] * states[-1] + fresh[k])
    entering = jnp.stack(states).astype(jnp.bfloat16)
    outer = jnp.einsum("nbi,bhpn->bihp", cb, entering, preferred_element_type=jnp.float32)
    return (inner + outer * carry_in[..., None]).reshape(count, heads * HDIM)


def shards(
    tokens,
    w_gate,
    w_xin,
    w_bc,
    w_dt,
    conv_x,
    conv_x_bias,
    conv_bc,
    conv_bc_bias,
    dt_bias,
    decay_rate,
    d_skip,
    norm_gain,
    w_out,
    lengths,
):
    seqs = lax.axis_size("seq")
    tens = lax.axis_size("tensor")
    here = lax.axis_index("seq")
    own, depth = tokens.shape[0], w_gate.shape[0]
    total = own * seqs * tens
    chans = w_gate.shape[1] // seqs
    heads = w_dt.shape[1] // seqs
    parts = w_bc.shape[1] // (seqs * GROUPS)
    small = jnp.concatenate(
        [
            w_bc.T.reshape(seqs, parts, GROUPS, depth)
            .transpose(0, 2, 1, 3)
            .reshape(seqs, parts * GROUPS, depth),
            w_dt.T.reshape(seqs, heads, depth),
            jnp.zeros((seqs, -(parts * GROUPS + heads) % 16, depth), jnp.bfloat16),
        ],
        axis=1,
    )
    gate, xin, small = project_in(tokens, w_gate, w_xin, small, seqs, tens // 2)
    docs = doc_ids(lengths, jnp.arange(total, dtype=jnp.int32))

    def mine(vector, width, axis=0):
        return lax.dynamic_slice_in_dim(vector, here * width, width, axis)

    xc = conv_full(xin, mine(conv_x, chans, 1), mine(conv_x_bias, chans), docs, 0)

    def grouped(vector):
        lead = vector.shape[:-1]
        vector = mine(vector, parts * GROUPS, len(lead)).reshape(lead + (parts, GROUPS))
        return jnp.swapaxes(vector, -1, -2).reshape(lead + (parts * GROUPS,))

    bcc = conv_full(small[: parts * GROUPS], grouped(conv_bc), grouped(conv_bc_bias), docs, 1)
    bcc = lax.all_to_all(bcc.reshape(GROUPS, parts, total), "tensor", 0, 0, tiled=True)
    bcc = lax.all_gather(bcc, "seq", axis=0).transpose(1, 0, 2, 3).reshape(2 * STATE, total)
    dtin = small[parts * GROUPS : parts * GROUPS + heads].T.astype(jnp.float32)
    dtv = jax.nn.softplus(dtin + mine(dt_bias, heads)[None, :])
    y = scan_heads(
        xc, dtv, mine(decay_rate, heads), bcc[:STATE], bcc[STATE:], docs, min(STRETCH, total)
    )
    y = y + jnp.repeat(mine(d_skip, heads), HDIM)[None, :] * xc.astype(jnp.float32)
    gated = (y * jax.nn.silu(gate.astype(jnp.float32))).astype(jnp.bfloat16)
    return project_out(gated, norm_gain, w_out, own, seqs, tens // 2)


def solution(mesh):
    seqs, tens = mesh.shape["seq"], mesh.shape["tensor"]
    heads = INNER // HDIM
    narrow = tens == GROUPS and heads % (seqs * tens) == 0 and 2 * STATE % (seqs * tens) == 0
    body = shards if narrow else shards_wide
    in_specs = (
        P(("seq", "tensor"), None),
        P("seq", "tensor"),
        P("seq", "tensor"),
        P("seq", "tensor"),
        P("seq", "tensor"),
        P(None, "tensor"),
        P("tensor"),
        P(None, "tensor"),
        P("tensor"),
        P("tensor"),
        P("tensor"),
        P("tensor"),
        P("tensor"),
        P("tensor", "seq"),
        P(),
    )
    out_specs = P(("seq", "tensor"), None)
    return jax.shard_map(body, mesh=mesh, in_specs=in_specs, out_specs=out_specs, check_vma=False)
```

```python
import jax
import jax.numpy as jnp
import numpy as np
from jax import lax
from jax.experimental import pallas as pl
from jax.experimental.pallas import tpu as pltpu
from jax.sharding import PartitionSpec as P

HDIM = 64
GROUPS = 8
STATE = 128
CONV = 4
STRETCH = 256
INNER = 8192


HIGH = lax.Precision.HIGHEST


def from_behind(x, axis, by):
    count = lax.axis_size(axis)
    pairs = [(i, i + by) for i in range(count) if 0 <= i + by < count]
    return lax.ppermute(x, axis, pairs)


def carried_in(x, axis, combine, identity):
    count, here = (lax.axis_size(axis), lax.axis_index(axis))
    everything = jax.tree.map(
        lambda part, kind: lax.all_gather(part.astype(kind), axis), x, (jnp.bfloat16, jnp.bfloat16)
    )
    start = jax.tree.map(
        lambda part, zero: jnp.broadcast_to(jnp.asarray(zero, part.dtype), part.shape), x, identity
    )

    def hop(k, before):
        reached = k < here
        new = combine(
            before, jax.tree.map(lambda part, own: part[k].astype(own.dtype), everything, x)
        )
        return jax.tree.map(lambda a, b: jnp.where(reached, a, b), new, before)

    return lax.fori_loop(0, count, hop, start)


def doc_ids(lengths, positions):
    starts = jnp.cumsum(lengths) - lengths
    counted = jnp.sum((starts[None, :] <= positions[:, None]).astype(jnp.int32), axis=1)
    return counted - 1


def causal_conv(values, edge, weights, bias, docs, edge_docs):
    count = values.shape[0]
    extended = jnp.concatenate([edge, values], axis=0).astype(jnp.float32)
    all_docs = jnp.concatenate([edge_docs, docs])
    summed = jnp.zeros(values.shape, jnp.float32) + bias[None, :]
    for offset in range(weights.shape[0]):
        same = (all_docs[offset : offset + count] == docs).astype(jnp.float32)
        summed = (
            summed + weights[offset][None, :] * extended[offset : offset + count] * same[:, None]
        )
    return lax.optimization_barrier(jax.nn.silu(summed).astype(jnp.bfloat16))


def ssd_blocks(xvals, dtv, rate, bmat, cmat, docs, prev_doc, head_group, block):
    count, heads, hdim = xvals.shape
    nstate = bmat.shape[2]
    blocks = count // block
    logs = -dtv * rate[None, :]

    def split(array):
        return array.reshape((blocks, block) + array.shape[1:])

    lower = jnp.tril(jnp.ones((block, block), bool))

    def step(carry, pieces):
        state, last_doc = carry
        xblk, dblk, lblk, bblk, cblk, docblk = pieces
        cum = jnp.cumsum(lblk, axis=0)
        same = (docblk[:, None] == docblk[None, :]) & lower
        diff = cum.T[:, :, None] - cum.T[:, None, :]
        decay = jnp.exp(jnp.where(same[None], diff, -jnp.inf))
        scores = jnp.einsum("ign,jgn->gij", cblk, bblk, precision=HIGH)
        mixing = scores[head_group] * decay * dblk.T[:, None, :]
        inner = jnp.einsum("hij,jhp->ihp", mixing, xblk, precision=HIGH)
        open_in = (docblk == last_doc).astype(jnp.float32)
        carry_in = jnp.exp(cum) * open_in[:, None]
        chead = cblk[:, head_group, :]
        outer = jnp.einsum("ihn,hpn->ihp", chead, state, precision=HIGH) * carry_in[:, :, None]
        end_doc = docblk[-1]
        tail = (
            jnp.exp(cum[-1][None, :] - cum)
            * (docblk == end_doc).astype(jnp.float32)[:, None]
            * dblk
        )
        bhead = bblk[:, head_group, :]
        fresh = jnp.einsum("jh,jhp,jhn->hpn", tail, xblk, bhead, precision=HIGH)
        state = carry_in[-1][:, None, None] * state + fresh
        return ((state, end_doc), inner + outer)

    init = (jnp.zeros((heads, hdim, nstate), jnp.float32), prev_doc)
    (state, end_doc), outs = lax.scan(
        step, init, (split(xvals), split(dtv), split(logs), split(bmat), split(cmat), split(docs))
    )
    return (outs.reshape(count, heads, hdim), state)


def shards_wide(
    tokens,
    w_gate,
    w_xin,
    w_bc,
    w_dt,
    conv_x,
    conv_x_bias,
    conv_bc,
    conv_bc_bias,
    dt_bias,
    decay_rate,
    d_skip,
    norm_gain,
    w_out,
    lengths,
):
    tensor_count = lax.axis_size("tensor")
    seq_index = lax.axis_index("seq")
    tensor_index = lax.axis_index("tensor")
    span_rows = lax.all_gather(tokens, "tensor", axis=0, tiled=True)
    span_len = span_rows.shape[0]
    pieces = (
        lax.all_gather(w_gate, "seq", axis=0, tiled=True),
        lax.all_gather(w_xin, "seq", axis=0, tiled=True),
        lax.all_gather(w_bc, "seq", axis=0, tiled=True),
        lax.all_gather(w_dt, "seq", axis=0, tiled=True),
    )
    gate_acc, xin_acc, bc_acc, dt_acc = tuple(
        (
            jnp.dot(span_rows, weight_piece, preferred_element_type=jnp.float32)
            for weight_piece in pieces
        )
    )
    gate = gate_acc.astype(jnp.bfloat16)
    xin = xin_acc.astype(jnp.bfloat16)
    bcin = bc_acc.astype(jnp.bfloat16)
    dtin = dt_acc.astype(jnp.bfloat16)
    gate, xin, bcin, dtin = lax.optimization_barrier((gate, xin, bcin, dtin))
    positions = seq_index * span_len + jnp.arange(span_len, dtype=jnp.int32)
    docs = doc_ids(lengths, positions)
    edge_docs = doc_ids(lengths, seq_index * span_len + jnp.arange(-(CONV - 1), 0, dtype=jnp.int32))
    prev_span_doc = doc_ids(lengths, positions[:1] - 1)[0]
    edge_x, edge_bc = from_behind(
        (xin[span_len - (CONV - 1) :], bcin[span_len - (CONV - 1) :]), "seq", 1
    )
    x_conv = causal_conv(xin, edge_x, conv_x, conv_x_bias, docs, edge_docs)
    bc_conv = causal_conv(bcin, edge_bc, conv_bc, conv_bc_bias, docs, edge_docs)
    group_span = tensor_count // GROUPS
    my_group = tensor_index // group_span
    every_group = lax.all_gather(bc_conv, "tensor", axis=1, tiled=True)
    arranged = every_group.reshape(span_len, 2 * STATE, GROUPS)
    group_cols = lax.dynamic_slice_in_dim(arranged, my_group, 1, 2).reshape(span_len, 2 * STATE)
    head_dev = w_dt.shape[1]
    head_group = np.zeros(head_dev, dtype=np.int32)
    both = group_cols.astype(jnp.float32)
    bmat = both[:, None, :STATE]
    cmat = both[:, None, STATE:]
    xvals = x_conv.astype(jnp.float32).reshape(span_len, head_dev, HDIM)
    dtv = jax.nn.softplus(dtin.astype(jnp.float32) + dt_bias[None, :])
    block = min(STRETCH, span_len)
    y_local, end_state = ssd_blocks(
        xvals, dtv, decay_rate, bmat, cmat, docs, prev_span_doc, head_group, block
    )
    cum_span = jnp.cumsum(-dtv * decay_rate[None, :], axis=0)
    open_span = (docs == prev_span_doc).astype(jnp.float32)
    span_decay = jnp.exp(cum_span[-1]) * open_span[-1]

    def combine(earlier, later):
        return (earlier[0] * later[0], later[0][:, None, None] * earlier[1] + later[1])

    entering = carried_in(
        (span_decay, end_state),
        "seq",
        combine,
        (jnp.ones_like(span_decay), jnp.zeros_like(end_state)),
    )[1]
    carried = jnp.exp(cum_span) * open_span[:, None]
    y_enter = (
        jnp.einsum("ihn,hpn->ihp", cmat[:, head_group, :], entering, precision=HIGH)
        * carried[:, :, None]
    )
    yvals = (y_local + y_enter + d_skip[None, :, None] * xvals).reshape(span_len, head_dev * HDIM)
    gated = yvals * jax.nn.silu(gate.astype(jnp.float32))
    local_sq = jnp.sum(gated * gated, axis=1)
    group_mark = (jnp.arange(GROUPS) == my_group).astype(jnp.float32)
    every_sum = lax.psum(local_sq[:, None] * group_mark[None, :], "tensor")
    group_mean = jnp.sum(every_sum * group_mark[None, :], axis=1) / (INNER // GROUPS)
    normed = (gated * lax.rsqrt(group_mean + 1e-05)[:, None] * norm_gain[None, :]).astype(
        jnp.bfloat16
    )
    w_full = lax.all_gather(w_out, "seq", axis=1, tiled=True)
    return lax.psum_scatter(
        jnp.dot(normed, w_full, preferred_element_type=jnp.float32).astype(jnp.bfloat16),
        "tensor",
        scatter_dimension=0,
        tiled=True,
    )


def enter(peers):
    barrier = pltpu.get_barrier_semaphore()
    for peer in peers:
        pl.semaphore_signal(barrier, inc=1, device_id=peer, device_id_type=pl.DeviceIdType.MESH)
    pl.semaphore_wait(barrier, len(peers))


def remote(src, dst, send, recv, peer):
    return pltpu.make_async_remote_copy(
        src_ref=src,
        dst_ref=dst,
        send_sem=send,
        recv_sem=recv,
        device_id=peer,
        device_id_type=pl.DeviceIdType.MESH,
    )


def places():
    s, t = lax.axis_index("seq"), lax.axis_index("tensor")
    seqs, chips = lax.axis_size("seq"), lax.axis_size("tensor") // 2
    z, c = t // 2, t % 2

    def along(ds, dz):
        return lax.rem(s + ds, seqs), lax.rem(z + dz, chips)

    return s, z, c, seqs, chips, along


def out_kernel(
    g_ref, gain_ref, w_ref, out_ref, held, normed, part, sib, pair, got,
    g_send, g_recv, p_send, p_recv, o_send, o_recv,
):
    s, z, c, seqs, chips, along = places()
    span = g_ref.shape[0] // seqs
    width = g_ref.shape[1]
    own = out_ref.shape[0]
    cols = w_ref.shape[1]
    sibling = (s, 2 * z + 1 - c)
    offsets = [(ds, dz) for ds in range(seqs) for dz in range(chips) if ds or dz]
    enter([(along(ds, dz)[0], 2 * along(ds, dz)[1] + c) for ds, dz in offsets] + [sibling])
    order = list(range(1, seqs)) + [0]
    gathers = {}
    for k in order:
        for ds in range(1, seqs):
            rows = pl.ds(pl.multiple_of(lax.rem(s + ds + k, seqs) * span, span), span)
            gathers[k, ds] = remote(
                g_ref.at[rows],
                held.at[ds, rows],
                g_send.at[k, ds],
                g_recv.at[k, ds],
                (along(ds, 0)[0], 2 * z + c),
            )
            gathers[k, ds].start()
    pairs, sends = {}, []

    def finish(k):
        q = lax.rem(s + k, seqs)
        pairs[k].wait_recv()
        for dz in range(chips):
            there = along(0, dz)[1]
            both = part[q, there, c].astype(jnp.float32) + sib[q, there].astype(jnp.float32)
            if k == 0 and dz == 0:
                got[0, 0] = both.astype(jnp.bfloat16)
            else:
                pair[k, dz] = both.astype(jnp.bfloat16)
                sends.append(
                    remote(
                        pair.at[k, dz],
                        got.at[k, dz],
                        o_send.at[k, dz],
                        o_recv.at[k, dz],
                        (q, 2 * there + c),
                    )
                )
                sends[-1].start()

    for step, k in enumerate(order):
        q = lax.rem(s + k, seqs)
        rows = pl.ds(pl.multiple_of(q * span, span), span)
        for ds in range(1, seqs):
            gathers[k, ds].wait_recv()
        blocks = [g_ref[rows, :].astype(jnp.float32)] + [
            held[ds, rows, :].astype(jnp.float32) for ds in range(1, seqs)
        ]
        squares = blocks[0] * blocks[0]
        for b in blocks[1:]:
            squares = squares + b * b
        scale = lax.rsqrt(jnp.sum(squares, axis=1, keepdims=True) / (width * seqs) + 1e-05)
        froms = [pl.multiple_of(lax.rem(s + seqs - ds, seqs) * width, width) for ds in range(seqs)]
        for ds in range(seqs):
            normed[ds] = (blocks[ds] * scale * gain_ref[:, pl.ds(froms[ds], width)]).astype(
                jnp.bfloat16
            )
        tile = 256

        def column(n, _):
            here = pl.ds(pl.multiple_of(n * tile, tile), tile)
            acc = jnp.zeros((span, tile), jnp.float32)
            for ds in range(seqs):
                acc = acc + jnp.dot(
                    normed[ds],
                    w_ref[pl.ds(froms[ds], width), here],
                    preferred_element_type=jnp.float32,
                )
            part[q, :, :, :, here] = acc.astype(jnp.bfloat16).reshape(chips, 2, own, tile)
            return 0

        lax.fori_loop(0, cols // tile, column, 0)
        pairs[k] = remote(
            part.at[q, :, 1 - c], sib.at[q], p_send.at[k], p_recv.at[k], sibling
        )
        pairs[k].start()
        if step:
            finish(order[step - 1])
    finish(order[-1])
    for copy in sends:
        copy.wait_recv()
    for ds in range(seqs):
        total = got[ds, 0].astype(jnp.float32)
        for dz in range(1, chips):
            total = total + got[ds, dz].astype(jnp.float32)
        begin = pl.multiple_of(lax.rem(s + seqs - ds, seqs) * cols, cols)
        out_ref[:, pl.ds(begin, cols)] = total.astype(jnp.bfloat16)
    for copy in list(gathers.values()) + list(pairs.values()) + sends:
        copy.wait_send()


def project_out(gated, gain, w_out, own, seqs, chips):
    total, width = gated.shape
    cols = w_out.shape[1]
    dma = pltpu.SemaphoreType.DMA
    vmem = pl.BlockSpec(memory_space=pltpu.VMEM)
    return pl.pallas_call(
        out_kernel,
        out_shape=jax.ShapeDtypeStruct((own, cols * seqs), jnp.bfloat16),
        in_specs=[vmem] * 3,
        out_specs=vmem,
        scratch_shapes=[
            pltpu.VMEM((seqs, total, width), jnp.bfloat16),
            pltpu.VMEM((seqs, total // seqs, width), jnp.bfloat16),
            pltpu.VMEM((seqs, chips, 2, own, cols), jnp.bfloat16),
            pltpu.VMEM((seqs, chips, own, cols), jnp.bfloat16),
            pltpu.VMEM((seqs, chips, own, cols), jnp.bfloat16),
            pltpu.VMEM((seqs, chips, own, cols), jnp.bfloat16),
            dma((seqs, seqs)),
            dma((seqs, seqs)),
            dma((seqs,)),
            dma((seqs,)),
            dma((seqs, chips)),
            dma((seqs, chips)),
        ],
        compiler_params=pltpu.CompilerParams(
            collective_id=1, has_side_effects=True, vmem_limit_bytes=40 * 2**20
        ),
    )(gated, gain[None, :], w_out)


def in_kernel(
    tok_ref, wg_ref, wx_ref, ws_ref, gate_ref, xin_ref, small_ref,
    tok, mine, mine_s, sent, sent_s, got, got_s,
    t_send, t_recv, f_send, f_recv, p_send, p_recv, q_send, q_recv,
):
    s, z, c, seqs, chips, along = places()
    own = tok_ref.shape[0]
    depth = wg_ref.shape[0]
    width = wg_ref.shape[1] // seqs
    span = own * chips * 2
    sibling = (s, 2 * z + 1 - c)
    offsets = [(ds, dz) for ds in range(seqs) for dz in range(chips) if ds or dz]
    enter([(along(ds, dz)[0], 2 * along(ds, dz)[1] + c) for ds, dz in offsets] + [sibling])
    spread = {}
    for ds, dz in offsets:
        to, there = along(ds, dz)
        spread[ds, dz] = remote(
            tok_ref.at[:, pl.ds(pl.multiple_of(to * depth, depth), depth)],
            tok.at[ds, z, c],
            t_send.at[ds, dz],
            t_recv.at[ds, dz],
            (to, 2 * there + c),
        )
        spread[ds, dz].start()
    tok[0, z, c] = tok_ref[:, pl.ds(pl.multiple_of(s * depth, depth), depth)]
    forwards, sums = [], []

    def forward(k):
        for ds, dz in offsets:
            if ds == k:
                spread[ds, dz].wait_recv()
        forwards.append(
            remote(tok.at[k, :, c], tok.at[k, :, c], f_send.at[k], f_recv.at[k], sibling)
        )
        forwards[k].start()

    forward(0)
    for k in range(seqs):
        forwards[k].wait_recv()
        if k + 1 < seqs:
            forward(k + 1)
        q = lax.rem(s + seqs - k, seqs)
        for ds in list(range(1, seqs)) + [0]:
            to = along(ds, 0)[0]
            cols = pl.ds(pl.multiple_of(to * width, width), width)
            rows = tok[k].reshape(span, depth)
            gate = jnp.dot(rows, wg_ref[:, cols], preferred_element_type=jnp.float32)
            xin = jnp.dot(rows, wx_ref[:, cols], preferred_element_type=jnp.float32)
            small = lax.dot_general(
                ws_ref[to], rows, (((1,), (1,)), ((), ())), preferred_element_type=jnp.float32
            )
            if ds == 0:
                mine[q, :, :width] = gate
                mine[q, :, width:] = xin
                mine_s[q] = small
                continue
            sent[ds, k, :, :width] = gate.astype(jnp.bfloat16)
            sent[ds, k, :, width:] = xin.astype(jnp.bfloat16)
            sent_s[ds, k] = small.astype(jnp.bfloat16)
            peer = (to, 2 * z + c)
            for copy in (
                remote(sent.at[ds, k], got.at[ds, q], p_send.at[ds, k], p_recv.at[ds, k], peer),
                remote(
                    sent_s.at[ds, k], got_s.at[ds, q], q_send.at[ds, k], q_recv.at[ds, k], peer
                ),
            ):
                copy.start()
                sums.append(copy)
    for copy in sums:
        copy.wait_recv()

    def add(q, _):
        rows = pl.ds(pl.multiple_of(q * span, span), span)
        total, small = mine[q], mine_s[q]
        for ds in range(1, seqs):
            total = total + got[ds, q].astype(jnp.float32)
            small = small + got_s[ds, q].astype(jnp.float32)
        gate_ref[rows, :] = total[:, :width].astype(jnp.bfloat16)
        xin_ref[rows, :] = total[:, width:].astype(jnp.bfloat16)
        small_ref[:, rows] = small.astype(jnp.bfloat16)
        return 0

    lax.fori_loop(0, seqs, add, 0)
    for copy in list(spread.values()) + forwards + sums:
        copy.wait_send()


def project_in(tokens, w_gate, w_xin, w_small, seqs, chips):
    own = tokens.shape[0]
    depth = w_gate.shape[0]
    width = w_gate.shape[1] // seqs
    span = own * chips * 2
    few = w_small.shape[1]
    dma = pltpu.SemaphoreType.DMA
    vmem = pl.BlockSpec(memory_space=pltpu.VMEM)
    return pl.pallas_call(
        in_kernel,
        out_shape=(
            jax.ShapeDtypeStruct((span * seqs, width), jnp.bfloat16),
            jax.ShapeDtypeStruct((span * seqs, width), jnp.bfloat16),
            jax.ShapeDtypeStruct((few, span * seqs), jnp.bfloat16),
        ),
        in_specs=[vmem] * 4,
        out_specs=(vmem,) * 3,
        scratch_shapes=[
            pltpu.VMEM((seqs, chips, 2, own, depth), jnp.bfloat16),
            pltpu.VMEM((seqs, span, 2 * width), jnp.float32),
            pltpu.VMEM((seqs, few, span), jnp.float32),
            pltpu.VMEM((seqs, seqs, span, 2 * width), jnp.bfloat16),
            pltpu.VMEM((seqs, seqs, few, span), jnp.bfloat16),
            pltpu.VMEM((seqs, seqs, span, 2 * width), jnp.bfloat16),
            pltpu.VMEM((seqs, seqs, few, span), jnp.bfloat16),
            dma((seqs, chips)),
            dma((seqs, chips)),
            dma((seqs,)),
            dma((seqs,)),
            dma((seqs, seqs)),
            dma((seqs, seqs)),
            dma((seqs, seqs)),
            dma((seqs, seqs)),
        ],
        compiler_params=pltpu.CompilerParams(
            collective_id=2, has_side_effects=True, vmem_limit_bytes=48 * 2**20
        ),
    )(tokens, w_gate, w_xin, w_small)


def group_kernel(in_ref, out_ref, held, t_send, t_recv, s_send, s_recv):
    s, t = lax.axis_index("seq"), lax.axis_index("tensor")
    seqs, tens = lax.axis_size("seq"), lax.axis_size("tensor")
    across = [(s, lax.rem(t + dt, tens)) for dt in range(1, tens)]
    along = [(lax.rem(s + ds, seqs), t) for ds in range(1, seqs)]
    enter(across + along)
    first = [
        remote(in_ref.at[peer[1]], held.at[0, t], t_send.at[dt], t_recv.at[dt], peer)
        for dt, peer in enumerate(across)
    ]
    for copy in first:
        copy.start()
    held[0, t] = in_ref[t]
    for copy in first:
        copy.wait_recv()
    second = [
        remote(held.at[0], held.at[1 + ds], s_send.at[ds], s_recv.at[ds], peer)
        for ds, peer in enumerate(along)
    ]
    for copy in second:
        copy.start()
    for copy in second:
        copy.wait_recv()
    out_ref[...] = held[...]
    for copy in first + second:
        copy.wait_send()


def to_groups(values, seqs):
    tens, rows, cols = values.shape
    dma = pltpu.SemaphoreType.DMA
    vmem = pl.BlockSpec(memory_space=pltpu.VMEM)
    return pl.pallas_call(
        group_kernel,
        out_shape=jax.ShapeDtypeStruct((seqs, tens, rows, cols), values.dtype),
        in_specs=[vmem],
        out_specs=vmem,
        scratch_shapes=[
            pltpu.VMEM((seqs, tens, rows, cols), values.dtype),
            dma((tens - 1,)),
            dma((tens - 1,)),
            dma((seqs - 1,)),
            dma((seqs - 1,)),
        ],
        compiler_params=pltpu.CompilerParams(
            collective_id=3, has_side_effects=True, vmem_limit_bytes=16 * 2**20
        ),
    )(values)


def conv_full(values, weights, bias, docs, axis):
    count = values.shape[axis]
    values = values.astype(jnp.float32)

    def along(vector):
        return vector[:, None] if axis == 0 else vector[None, :]

    def across(vector):
        return vector[None, :] if axis == 0 else vector[:, None]

    summed = across(weights[CONV - 1]) * values + across(bias)
    for back in range(1, CONV):
        kept = lax.slice_in_dim(values, 0, count - back, axis=axis)
        pad = [(0, 0), (0, 0)]
        pad[axis] = (back, 0)
        same = jnp.concatenate(
            [jnp.zeros((back,), jnp.float32), (docs[:-back] == docs[back:]).astype(jnp.float32)]
        )
        summed = summed + across(weights[CONV - 1 - back]) * jnp.pad(kept, pad) * along(same)
    return jax.nn.silu(summed).astype(jnp.bfloat16)


def scan_heads(xc, dtv, rate, bmat, cmat, docs, block):
    count, heads = dtv.shape
    blocks = count // block
    xh = xc.reshape(blocks, block, heads, HDIM)
    dtb = dtv.reshape(blocks, block, heads)
    upto = jnp.tril(jnp.ones((block, block), jnp.float32))
    cum = jnp.einsum("ij,bjh->bih", upto, -dtb * rate[None, None, :], precision=HIGH)
    docb = docs.reshape(blocks, block)
    bb = bmat.reshape(STATE, blocks, block)
    cb = cmat.reshape(STATE, blocks, block)
    scores = jnp.einsum("nbi,nbj->bij", cb, bb, preferred_element_type=jnp.float32)
    lower = jnp.tril(jnp.ones((block, block), bool))
    same = (docb[:, :, None] == docb[:, None, :]) & lower[None]
    cumt = cum.transpose(0, 2, 1)
    diff = cumt[:, :, :, None] - cumt[:, :, None, :]
    decay = jnp.exp(jnp.where(same[:, None], diff, -jnp.inf))
    mixing = scores[:, None] * decay * dtb.transpose(0, 2, 1)[:, :, None, :]
    inner = jnp.einsum(
        "bhij,bjhp->bihp", mixing.astype(jnp.bfloat16), xh, preferred_element_type=jnp.float32
    )
    end_doc = docb[:, -1]
    last_doc = jnp.concatenate([jnp.full((1,), -1, docs.dtype), end_doc[:-1]])
    carry_in = jnp.exp(cum) * (docb == last_doc[:, None]).astype(jnp.float32)[:, :, None]
    tail = jnp.exp(cum[:, -1:] - cum) * (docb == end_doc[:, None]).astype(jnp.float32)[:, :, None] * dtb
    tx = (tail[..., None] * xh.astype(jnp.float32)).astype(jnp.bfloat16)
    fresh = jnp.einsum("bjhp,nbj->bhpn", tx, bb, preferred_element_type=jnp.float32)
    states = [jnp.zeros((heads, HDIM, STATE), jnp.float32)]
    for k in range(blocks - 1):
        states.append(carry_in[k, -1][:, None, None] * states[-1] + fresh[k])
    entering = jnp.stack(states).astype(jnp.bfloat16)
    outer = jnp.einsum("nbi,bhpn->bihp", cb, entering, preferred_element_type=jnp.float32)
    return (inner + outer * carry_in[..., None]).reshape(count, heads * HDIM)


def shards(
    tokens,
    w_gate,
    w_xin,
    w_bc,
    w_dt,
    conv_x,
    conv_x_bias,
    conv_bc,
    conv_bc_bias,
    dt_bias,
    decay_rate,
    d_skip,
    norm_gain,
    w_out,
    lengths,
):
    seqs = lax.axis_size("seq")
    tens = lax.axis_size("tensor")
    here = lax.axis_index("seq")
    own, depth = tokens.shape[0], w_gate.shape[0]
    total = own * seqs * tens
    chans = w_gate.shape[1] // seqs
    heads = w_dt.shape[1] // seqs
    parts = w_bc.shape[1] // (seqs * GROUPS)
    small = jnp.concatenate(
        [
            w_bc.T.reshape(seqs, parts, GROUPS, depth)
            .transpose(0, 2, 1, 3)
            .reshape(seqs, parts * GROUPS, depth),
            w_dt.T.reshape(seqs, heads, depth),
            jnp.zeros((seqs, -(parts * GROUPS + heads) % 16, depth), jnp.bfloat16),
        ],
        axis=1,
    )
    gate, xin, small = project_in(tokens, w_gate, w_xin, small, seqs, tens // 2)
    docs = doc_ids(lengths, jnp.arange(total, dtype=jnp.int32))

    def mine(vector, width, axis=0):
        return lax.dynamic_slice_in_dim(vector, here * width, width, axis)

    xc = conv_full(xin, mine(conv_x, chans, 1), mine(conv_x_bias, chans), docs, 0)

    def grouped(vector):
        lead = vector.shape[:-1]
        vector = mine(vector, parts * GROUPS, len(lead)).reshape(lead + (parts, GROUPS))
        return jnp.swapaxes(vector, -1, -2).reshape(lead + (parts * GROUPS,))

    bcc = conv_full(small[: parts * GROUPS], grouped(conv_bc), grouped(conv_bc_bias), docs, 1)
    fold = 16 // parts
    bcc = bcc.reshape(GROUPS, parts, fold, total // fold).transpose(0, 2, 1, 3)
    bcc = to_groups(bcc.reshape(GROUPS, 16, total // fold), seqs)
    bcc = bcc.reshape(seqs, tens, fold, parts, total // fold).transpose(1, 0, 3, 2, 4)
    bcc = bcc.reshape(2 * STATE, total)
    dtin = small[parts * GROUPS : parts * GROUPS + heads].T.astype(jnp.float32)
    dtv = jax.nn.softplus(dtin + mine(dt_bias, heads)[None, :])
    y = scan_heads(
        xc, dtv, mine(decay_rate, heads), bcc[:STATE], bcc[STATE:], docs, min(STRETCH, total)
    )
    y = y + jnp.repeat(mine(d_skip, heads), HDIM)[None, :] * xc.astype(jnp.float32)
    gated = (y * jax.nn.silu(gate.astype(jnp.float32))).astype(jnp.bfloat16)
    return project_out(gated, norm_gain, w_out, own, seqs, tens // 2)


def solution(mesh):
    seqs, tens = mesh.shape["seq"], mesh.shape["tensor"]
    heads = INNER // HDIM
    narrow = tens == GROUPS and heads % (seqs * tens) == 0 and 2 * STATE == 8 * seqs * tens
    body = shards if narrow else shards_wide
    in_specs = (
        P(("seq", "tensor"), None),
        P("seq", "tensor"),
        P("seq", "tensor"),
        P("seq", "tensor"),
        P("seq", "tensor"),
        P(None, "tensor"),
        P("tensor"),
        P(None, "tensor"),
        P("tensor"),
        P("tensor"),
        P("tensor"),
        P("tensor"),
        P("tensor"),
        P("tensor", "seq"),
        P(),
    )
    out_specs = P(("seq", "tensor"), None)
    return jax.shard_map(body, mesh=mesh, in_specs=in_specs, out_specs=out_specs, check_vma=False)
```
